32 devices in a mesh: groups: 2 (over x), ep: 16 (over z, y, core).
Axes of the slice: x: 2, y: 2, z: 4, core: 2. Of those that a mesh axis runs over, the one named last changes fastest.
Arguments:
- query_proj: bfloat16 [8192, 4096], P(('groups', 'ep')), parts along dimension 0, may hold values from -8 to 8
- key_proj: bfloat16 [8192, 512], P(('groups', 'ep')), parts along dimension 0, may hold values from -8 to 8
- value_proj: bfloat16 [8192, 512], P(('groups', 'ep')), parts along dimension 0, may hold values from -6 to 6
- call_ids: int32 [8192], P(('groups', 'ep')), parts along dimension 0, may hold values from 0 to 15, never falling along the last dimension, each value on 1 to 1024 neighbouring positions
- sink_logits: float32 [64], replicated, may hold values from 2 to 6
- routed_stream: bfloat16 [512, 2880], P(('groups', 'ep')), parts along dimension 0, may hold values from -6 to 6
- expert_ids: int32 [512, 4], P(('groups', 'ep')), parts along dimension 0, may hold values from 0 to 7, as said below
- route_weights: float32 [512, 4], P(('groups', 'ep')), parts along dimension 0, may hold values from 0.1 to 1
- gate_up: bfloat16 [16, 2880, 2880], P('ep'), may hold values from -0.109375 to 0.109375
- down_proj: bfloat16 [16, 1440, 2880], P('ep'), may hold values from -0.109375 to 0.109375
Outputs:
- attended: bfloat16 [8192, 4096], P(('groups', 'ep')), parts along dimension 0
- expert_mix: bfloat16 [512, 2880], P(('groups', 'ep')), parts along dimension 0
The draws below stay inside these ranges and needn't reach their ends.
There are 2 independent parts, one for each index of `groups`. The reference program is written for one: setup_inputs(seed, part) draws one part's arguments, and reference() takes and returns one part's arrays. A program takes and returns all parts, laid end to end along the dimension named above; an argument that names none is the same for every part. Nothing has to cross between parts.
Inputs may be any that keep to these rules, and one draw needn't show every extreme that they name: `expert_ids`: each row names 4 different experts. In each aligned block of 16 rows (the rows of one device) no expert is named by more than 12 rows, and some expert is named by exactly 12 rows in every block.
All inputs are finite; a program needn't handle non-finite values.
Results may differ from the reference program's by a relative error of at most 0.0058.
Values may be sent and summed in bfloat16 or wider, within the bound.
A program may use at most 128 MiB of HBM per device.

```python
import math
import jax
import jax.numpy as jnp
import numpy as np
from jax import lax

D = 2880
HQ = 64
HK = 8
HD = 64
WINDOW = 128
TOPK = 4
EXP_HIDDEN = 2880
EXPERTS = 8
TOK_DEV = 256
MOE_DEV = 16
SHARDS = 2
FE = 1440
SEQ = 4096
MOE_TOKENS = 256
CAP = 12
CALLS = 16
LONGEST = 1024


def draw_key_proj(key, part):
    baseline = jax.random.normal(jax.random.fold_in(key, 3), (SEQ, HK * HD), jnp.float32)
    return baseline.astype(jnp.bfloat16)


def draw_query_proj(key, part):
    baseline = jax.random.normal(jax.random.fold_in(key, 5), (SEQ, HQ * HD), jnp.float32)
    return baseline.astype(jnp.bfloat16)


def draw_expert_ids(key, part):
    blocks = MOE_TOKENS // MOE_DEV
    pick_count = MOE_DEV * TOPK
    hottest = jax.random.randint(jax.random.fold_in(key, 1), (), 0, EXPERTS)
    heat = jax.random.randint(jax.random.fold_in(key, 2), (EXPERTS,), 1, 5)
    owners = jnp.arange(EXPERTS, dtype=jnp.int32)

    def one_block(block_key):
        noise = jax.random.randint(jax.random.fold_in(block_key, 1), (EXPERTS, CAP), 0, 64)
        slot_rank = jnp.arange(CAP, dtype=jnp.int32)[None, :]
        scores = slot_rank * heat[:, None] * 64 + noise + 1
        scores = jnp.where(owners[:, None] == hottest, 0, scores)
        distinct = scores.reshape(-1) * (EXPERTS * CAP) + jnp.arange(EXPERTS * CAP, dtype=jnp.int32)
        order = jnp.argsort(distinct)
        chosen = jnp.zeros((EXPERTS * CAP,), jnp.int32).at[order[:pick_count]].set(1)
        counts = jnp.sum(chosen.reshape(EXPERTS, CAP), axis=1)
        cumulative = jnp.cumsum(counts)
        positions = jnp.arange(pick_count, dtype=jnp.int32)
        sorted_ids = jnp.sum((cumulative[None, :] <= positions[:, None]).astype(jnp.int32), axis=1)
        table = sorted_ids.reshape(TOPK, MOE_DEV).T
        shuffle = jax.random.permutation(jax.random.fold_in(block_key, 2), MOE_DEV)
        return table[shuffle]
    block_keys = jax.random.split(jax.random.fold_in(key, 4), blocks)
    return jax.vmap(one_block)(block_keys).reshape(MOE_TOKENS, TOPK).astype(jnp.int32)


def levels(rng, shape, shards, least, top_value):
    def one(axis_at, blocks):
        draws = jax.random.uniform(jax.random.fold_in(jax.random.fold_in(rng, 6), axis_at), (blocks,), jnp.float32, least / len(shards), top_value / len(shards))
        return jnp.repeat(jnp.exp(draws), shape[axis_at] // blocks).reshape((-1,) + (1,) * (len(shape) - axis_at - 1))

    factor_of = one(*shards[0])
    for cut in shards[1:]:
        factor_of = factor_of * one(*cut)
    return factor_of


def split_up(amount, total, limit, lean):
    portions = [(1 << 20) // math.isqrt(grade ** lean) + 1 for grade in range(2, amount + 1)]
    rest, given = total - limit - (amount - 1), [1] * (amount - 1)
    while rest > 0:
        free = [i for i in range(amount - 1) if given[i] < limit]
        pool, left = sum([portions[i] for i in free]), rest
        for i in free:
            more = min(limit - given[i], max(1, left * portions[i] // pool), rest)
            given[i] = given[i] + more
            rest = rest - more
    return np.array([limit] + given)


def ragged(own_key, amount, total, limit, skew):
    if amount == 2:
        one = jax.random.randint(own_key, (), max(1, total - limit), min(limit, total - 1) + 1)
        return jnp.stack([one, total - one])
    sizes = jnp.asarray(split_up(amount, total, limit, skew), jnp.int32)
    couples = (amount - 1) // 2
    source_of, receiver = sizes[1:1 + 2 * couples:2], sizes[2:2 + 2 * couples:2]
    margin = jnp.minimum(source_of - 1, limit - receiver)
    moved = jax.random.randint(jax.random.fold_in(own_key, 1), (couples,), 0, 1 << 20) % (margin + 1)
    sizes = sizes.at[1:1 + 2 * couples:2].set(source_of - moved).at[2:2 + 2 * couples:2].set(receiver + moved)
    return sizes[jax.random.permutation(jax.random.fold_in(own_key, 2), amount)]


def scatter_about(key, shape, deviation, bound, shards=(), kind=jnp.bfloat16):
    factor_of = levels(key, shape, shards, -0.22, 0.18) if shards else 1.0
    result = jax.random.normal(key, shape, jnp.float32) * deviation * factor_of
    return jnp.minimum(jnp.maximum(result, -bound), bound).astype(kind)


def setup_inputs(seed: int = 0, part: int = 0) -> dict:
    arg_keys = jax.random.split(jax.random.key(seed), 11)
    own_keys = jax.random.split(jax.random.fold_in(arg_keys[10], part), 11)
    return {
        "query_proj": draw_query_proj(jax.random.fold_in(jax.random.fold_in(arg_keys[10], part), 71), part),
        "key_proj": draw_key_proj(jax.random.fold_in(jax.random.fold_in(arg_keys[10], part), 71), part),
        "value_proj": scatter_about(own_keys[2], (SEQ, HK * HD), 1.0, 6.0, ((0, 16),)),
        "call_ids": jnp.searchsorted(jnp.cumsum(ragged(own_keys[3], CALLS, SEQ, LONGEST, 2)), jnp.arange(SEQ), side="right").astype(jnp.int32),
        "sink_logits": jnp.clip(jax.random.uniform(arg_keys[4], (HQ,), jnp.float32, 2.0, 6.0), 2.0, 6.0),
        "routed_stream": scatter_about(own_keys[5], (MOE_TOKENS, D), 1.0, 6.0, ((0, 16),)),
        "expert_ids": draw_expert_ids(jax.random.fold_in(jax.random.fold_in(arg_keys[10], part), 71), part),
        "route_weights": jnp.clip(0.1 + 0.9 * jax.random.uniform(own_keys[7], (MOE_TOKENS, TOPK), jnp.float32) ** levels(own_keys[7], (MOE_TOKENS, TOPK), ((0, 16),), -0.2, 0.2), 0.1, 1.0),
        "gate_up": scatter_about(arg_keys[8], (EXPERTS * SHARDS, D, 2 * FE), D ** -0.5, 0.109375, ((0, 16),)),
        "down_proj": scatter_about(arg_keys[9], (EXPERTS * SHARDS, FE, D), EXP_HIDDEN ** -0.5, 0.109375, ((0, 16),)),
    }


def window_block(query_block, key_block, value_block, query_calls, key_calls, sink_logits):
    length = query_block.shape[0]
    extent = key_block.shape[0]
    group_size = HQ // HK
    query_heads = query_block.astype(jnp.float32).reshape(length, HK, group_size, HD)
    key_heads = key_block.astype(jnp.float32).reshape(extent, HK, HD)
    value_heads = value_block.astype(jnp.float32).reshape(extent, HK, HD)
    scores = jnp.einsum("tkgd,skd->kgts", query_heads, key_heads) * (HD ** -0.5)
    query_pos = jnp.arange(length, dtype=jnp.int32) + (extent - length)
    key_pos = jnp.arange(extent, dtype=jnp.int32)
    visible = (key_pos[None, :] <= query_pos[:, None]) & (query_pos[:, None] - key_pos[None, :] < WINDOW) & (key_calls[None, :] == query_calls[:, None])
    scores = jnp.where(visible[None, None], scores, -1e30)
    sink_row = sink_logits.reshape(HK, group_size)[:, :, None]
    largest = jnp.maximum(jnp.max(scores, axis=-1), sink_row)
    weights = jnp.where(visible[None, None], jnp.exp(scores - largest[..., None]), 0.0)
    denominator = jnp.sum(weights, axis=-1) + jnp.exp(sink_row - largest)
    rounded = lax.optimization_barrier(weights.astype(jnp.bfloat16)).astype(jnp.float32)
    blended = jnp.einsum("kgts,skd->tkgd", rounded, value_heads)
    blended = blended / jnp.transpose(denominator, (2, 0, 1))[..., None]
    return blended.reshape(length, HQ * HD).astype(jnp.bfloat16)


def expert_rows(row_block, weight_in, weight_out):
    projected = jnp.dot(row_block, weight_in, preferred_element_type=jnp.float32)
    gate_part = projected[:, :FE]
    up_part = projected[:, FE:]
    activated = ((up_part + 1.0) * gate_part * jax.nn.sigmoid(1.702 * gate_part)).astype(jnp.bfloat16)
    return jnp.dot(activated, weight_out, preferred_element_type=jnp.float32).astype(jnp.bfloat16)


def block_slots(block_ids):
    flat_ids = block_ids.reshape(-1)
    owners = jnp.arange(EXPERTS, dtype=jnp.int32)
    onehot = (flat_ids[:, None] == owners[None, :]).astype(jnp.int32)
    pick_rank = jnp.sum((jnp.cumsum(onehot, axis=0) - onehot) * onehot, axis=1)
    return pick_rank.astype(jnp.int32)


def reference(query_proj, key_proj, value_proj, call_ids, sink_logits, routed_stream, expert_ids, route_weights, gate_up, down_proj):
    blocks = SEQ // TOK_DEV
    key_pad = jnp.concatenate([jnp.zeros((WINDOW, HK * HD), key_proj.dtype), key_proj], axis=0)
    value_pad = jnp.concatenate([jnp.zeros((WINDOW, HK * HD), value_proj.dtype), value_proj], axis=0)
    own_calls = (call_ids + 1).astype(jnp.int32)
    call_pad = jnp.concatenate([jnp.zeros((WINDOW,), jnp.int32), own_calls], axis=0)

    def one_block(block_index):
        offset = block_index * TOK_DEV
        return window_block(
            lax.dynamic_slice_in_dim(query_proj, offset, TOK_DEV, 0),
            lax.dynamic_slice_in_dim(key_pad, offset, TOK_DEV + WINDOW, 0),
            lax.dynamic_slice_in_dim(value_pad, offset, TOK_DEV + WINDOW, 0),
            lax.dynamic_slice_in_dim(own_calls, offset, TOK_DEV, 0),
            lax.dynamic_slice_in_dim(call_pad, offset, TOK_DEV + WINDOW, 0),
            sink_logits)

    attended = lax.map(one_block, jnp.arange(blocks, dtype=jnp.int32)).reshape(SEQ, HQ * HD)

    source_count = MOE_TOKENS // MOE_DEV
    pick_count = MOE_DEV * TOPK
    block_ids = expert_ids.reshape(source_count, pick_count)
    pick_rank = jax.vmap(block_slots)(block_ids)
    slot_of = block_ids * CAP + pick_rank
    source_rows = jnp.arange(source_count, dtype=jnp.int32)[:, None]
    tokens_global = (jnp.arange(pick_count, dtype=jnp.int32) // TOPK)[None, :] + source_rows * MOE_DEV
    sources = jnp.full((source_count, EXPERTS * CAP), MOE_TOKENS, jnp.int32)
    sources = sources.at[jnp.broadcast_to(source_rows, slot_of.shape), slot_of].set(tokens_global)
    by_expert = sources.reshape(source_count, EXPERTS, CAP).transpose(1, 0, 2).reshape(EXPERTS, source_count * CAP)
    padded = jnp.concatenate([routed_stream, jnp.zeros((1, D), routed_stream.dtype)], axis=0)
    gate_shards = gate_up.reshape(EXPERTS, SHARDS, D, 2 * FE)
    down_shards = down_proj.reshape(EXPERTS, SHARDS, FE, D)

    def one_expert(packed):
        rows = padded[packed[0]]

        def one_shard(weights_pair):
            return expert_rows(rows, weights_pair[0], weights_pair[1])

        partials = lax.map(one_shard, (packed[1], packed[2]))
        return jnp.sum(partials.astype(jnp.float32), axis=0)

    outputs = lax.map(one_expert, (by_expert, gate_shards, down_shards))
    position = source_rows * CAP + pick_rank
    picked = outputs[block_ids, position].reshape(MOE_TOKENS, TOPK, D)
    expert_mix = jnp.sum(route_weights[..., None] * picked, axis=1).astype(jnp.bfloat16)
    return attended, expert_mix
```

```python
import functools

import jax
import jax.numpy as jnp
from jax import lax
from jax.experimental import pallas as pl
from jax.experimental.pallas import tpu as pltpu
from jax.sharding import PartitionSpec as P

HD = 64
WINDOW = 128
EXPERTS = 8
LANES = 128
TILE = 256
F32 = jnp.float32
BF16 = jnp.bfloat16


def up_to(value, unit):
    return -(-value // unit) * unit


def cuts(total, width):
    return [(at, min(width, total - at)) for at in range(0, total, width)]


def row_parts(rows, parts):
    step = up_to(-(-rows // parts), 16)
    return cuts(rows, step)


def kernel(
    n,
    q_hbm,
    k_hbm,
    v_hbm,
    calls_ref,
    sink_ref,
    routed_ref,
    ids_ref,
    route_ref,
    gate_hbm,
    down_hbm,
    att_hbm,
    mix_ref,
    q_buf,
    o_buf,
    k_cat,
    v_cat,
    calls_in,
    calls_out,
    bias,
    tokens,
    w_in,
    w_out,
    hidden,
    act,
    mine,
    s1,
    r1,
    acc2,
    s2,
    r2,
    acc3,
    s3,
    r3,
    load_sem,
    gate_sem,
    down_sem,
    halo_send,
    halo_recv,
    z_send,
    y_send,
    c_send,
    slot_recv,
    s1_send,
    s1_recv,
    s2_send,
    s2_recv,
    s3_send,
    s3_recv,
    out_sem,
):
    zs = n // 4
    me = lax.axis_index("ep")
    core, row, z = me % 2, (me // 2) % 2, me // 4
    sibling = me + 1 - 2 * core
    across = me + 2 - 4 * row
    ahead, behind = (me + 1) % n, (me + n - 1) % n

    def along(by):
        return ((z + by) % zs) * 4 + row * 2 + core

    length = q_hbm.shape[0]
    block = length // 2
    count, d = routed_ref.shape
    dp = tokens.shape[1]
    fe = down_hbm.shape[0]
    half = zs * 2 * count
    quarter = zs * count

    barrier = pltpu.get_barrier_semaphore()
    for peer in [sibling, across, ahead, behind] + [along(k) for k in range(1, zs)]:
        pl.semaphore_signal(
            barrier, inc=1, device_id={"ep": peer}, device_id_type=pl.DeviceIdType.MESH
        )

    def remote(src, dst, send, recv, peer):
        return pltpu.make_async_remote_copy(
            src_ref=src,
            dst_ref=dst,
            send_sem=send,
            recv_sem=recv,
            device_id={"ep": peer},
            device_id_type=pl.DeviceIdType.MESH,
        )

    loads = [
        pltpu.make_async_copy(k_hbm, k_cat.at[pl.ds(WINDOW, length)], load_sem.at[0]),
        pltpu.make_async_copy(v_hbm, v_cat.at[pl.ds(WINDOW, length)], load_sem.at[1]),
        pltpu.make_async_copy(
            q_hbm.at[pl.ds(block, block)], q_buf.at[pl.ds(block, block)], load_sem.at[2]
        ),
        pltpu.make_async_copy(
            q_hbm.at[pl.ds(0, block)], q_buf.at[pl.ds(0, block)], load_sem.at[3]
        ),
    ]
    for copy in loads:
        copy.start()
    gate_loads = [
        pltpu.make_async_copy(
            gate_hbm.at[pl.ds(at, size)], w_in.at[pl.ds(at, size)], gate_sem.at[i]
        )
        for i, (at, size) in enumerate(row_parts(d, 4))
    ]
    down_loads = [
        pltpu.make_async_copy(
            down_hbm.at[pl.ds(at, size)], w_out.at[pl.ds(at, size)], down_sem.at[i]
        )
        for i, (at, size) in enumerate(row_parts(fe, 2))
    ]
    for copy in gate_loads + down_loads:
        copy.start()

    ids = ids_ref[...]
    route = route_ref[...]
    lane = lax.broadcasted_iota(jnp.int32, (count, LANES), 1)
    last = dp - LANES
    free = d - last
    extra = jnp.zeros((count, LANES), F32)
    for e in range(EXPERTS):
        weight = jnp.sum(jnp.where(ids == e, route, 0.0), axis=1, keepdims=True)
        high = weight.astype(BF16).astype(F32)
        extra = jnp.where(lane == free + e, high, extra)
        extra = jnp.where(lane == free + EXPERTS + e, weight - high, extra)
    tokens[0:count, 0:d] = routed_ref[...]
    tail = tokens[0:count, last:dp].astype(F32)
    tokens[0:count, last:dp] = jnp.where(lane < free, tail, extra).astype(BF16)
    own_calls = calls_ref[...]
    calls_out[...] = jnp.broadcast_to(own_calls[:, length - WINDOW :], calls_out.shape)

    pl.semaphore_wait(barrier, zs + 3)

    def slot(cr, yr, zr):
        return tokens.at[pl.ds(((cr * 2 + yr) * zs + zr) * count, count)]

    def arrival(cr, yr, zr):
        return slot_recv.at[(cr * 2 + yr) * zs + zr]

    sent = []

    def send(*args):
        copy = remote(*args)
        copy.start()
        sent.append(copy)

    def arrived(ref, sem):
        pltpu.make_async_copy(ref, ref, sem).wait()

    for k in range(1, zs):
        send(slot(0, 0, 0), slot(0, 0, zs - k), z_send.at[k - 1], arrival(0, 0, zs - k), along(k))
    send(slot(0, 0, 0), slot(0, 1, 0), y_send.at[0], arrival(0, 1, 0), across)
    send(slot(0, 0, 0), slot(1, 0, 0), c_send.at[0], arrival(1, 0, 0), sibling)
    edge = pl.ds(length - WINDOW, WINDOW)
    head = pl.ds(0, WINDOW)
    send(k_hbm.at[edge], k_cat.at[head], halo_send.at[0], halo_recv.at[0], ahead)
    send(v_hbm.at[edge], v_cat.at[head], halo_send.at[1], halo_recv.at[1], ahead)
    send(calls_out, calls_in, halo_send.at[2], halo_recv.at[2], ahead)

    def make_bias(index, key_calls, query_calls, behind_ok):
        query = lax.broadcasted_iota(jnp.int32, (block, WINDOW + block), 0)
        key = lax.broadcasted_iota(jnp.int32, (block, WINDOW + block), 1)
        spread = jnp.broadcast_to(query_calls, (block, block))
        diag = lax.broadcasted_iota(jnp.int32, (block, block), 0) == lax.broadcasted_iota(
            jnp.int32, (block, block), 1
        )
        column = jnp.sum(
            jnp.where(diag, spread.astype(F32), 0.0), axis=1, keepdims=True
        ).astype(jnp.int32)
        seen = (key <= query + WINDOW) & (key > query) & (key_calls == column)
        if behind_ok is not None:
            seen = seen & ((key >= WINDOW) | behind_ok)
        bias[index] = jnp.where(seen, 0.0, -1e30)

    def attend(index, first, stop):
        base = index * block
        span = WINDOW + block

        def body(gp, carry):
            columns = pl.ds(pl.multiple_of(gp * LANES, LANES), LANES)
            k2 = k_cat[base : base + span, columns].astype(F32) * HD ** (-0.5)
            v2 = v_cat[base : base + span, columns].astype(F32)
            low = lax.broadcasted_iota(jnp.int32, (span, LANES), 1) < HD
            low_out = lax.broadcasted_iota(jnp.int32, (block, LANES), 1) < HD
            ones_low = jnp.where(low, 1.0, 0.0)
            ones_high = 1.0 - ones_low
            for side in range(2):
                keep = low if side == 0 else jnp.logical_not(low)
                ka = jnp.where(keep, k2, 0.0)
                kb = pltpu.roll(ka, HD, 1)
                va = jnp.where(keep, v2, 0.0)
                vb = pltpu.roll(va, HD, 1)
                if side:
                    ka, kb, va, vb = kb, ka, vb, va
                keys = jnp.concatenate([ka, kb], axis=0).astype(BF16)
                values = jnp.concatenate(
                    [
                        jnp.concatenate([va, ones_low], axis=1),
                        jnp.concatenate([vb, ones_high], axis=1),
                    ],
                    axis=0,
                ).astype(BF16)
                for pair in range(4):
                    at = pl.multiple_of(gp * (16 * HD) + (side * 8 + pair * 2) * HD, LANES)
                    q2 = q_buf[base : base + block, pl.ds(at, LANES)]
                    scores = lax.dot_general(
                        q2, keys, (((1,), (1,)), ((), ())), preferred_element_type=F32
                    )
                    seen = bias[index]
                    weights, sinks = [], []
                    for one in range(2):
                        sink = sink_ref[gp * 16 + side * 8 + pair * 2 + one]
                        part = scores[:, one * span : (one + 1) * span] + seen
                        largest = jnp.maximum(jnp.max(part, axis=1, keepdims=True), sink)
                        weights.append(jnp.exp(part - largest))
                        sinks.append(jnp.exp(sink - largest))
                    both = jnp.concatenate(weights, axis=1).astype(BF16)
                    mixed = jnp.dot(both, values, preferred_element_type=F32)
                    bottom = mixed[:, LANES:] + jnp.where(low_out, sinks[0], sinks[1])
                    o_buf[base : base + block, pl.ds(at, LANES)] = (
                        mixed[:, :LANES] / bottom
                    ).astype(BF16)
            return carry

        lax.fori_loop(first, stop, body, 0)

    groups = k_hbm.shape[1] // LANES
    make_bias(1, own_calls, own_calls[:, block:], None)
    for copy in loads[:3]:
        copy.wait()
    attend(1, 0, groups // 2)
    for k in range(1, zs):
        arrived(slot(0, 0, zs - k), arrival(0, 0, zs - k))
        send(slot(0, 0, zs - k), slot(0, 1, zs - k), y_send.at[k], arrival(0, 1, zs - k), across)
        send(slot(0, 0, zs - k), slot(1, 0, zs - k), c_send.at[k], arrival(1, 0, zs - k), sibling)
    attend(1, groups // 2, groups)
    store_late = pltpu.make_async_copy(
        o_buf.at[pl.ds(block, block)], att_hbm.at[pl.ds(block, block)], out_sem.at[0]
    )
    store_late.start()
    for k in range(zs):
        zr = (zs - k) % zs
        arrived(slot(0, 1, zr), arrival(0, 1, zr))
        send(slot(0, 1, zr), slot(1, 1, zr), c_send.at[zs + k], arrival(1, 1, zr), sibling)
    for copy in gate_loads + down_loads:
        copy.wait()
    loads[3].wait()
    arrived(k_cat.at[head], halo_recv.at[0])
    arrived(v_cat.at[head], halo_recv.at[1])
    arrived(calls_in, halo_recv.at[2])
    make_bias(
        0,
        jnp.concatenate([calls_in[0:1, :], own_calls[:, :block]], axis=1),
        own_calls[:, :block],
        me > 0,
    )
    for yr in range(2):
        for zr in range(zs):
            arrived(slot(1, yr, zr), arrival(1, yr, zr))

    rows = n * count

    def project(at, size):
        hidden[:, pl.ds(at, size)] = jnp.dot(
            tokens[:, 0:d], w_in[:, pl.ds(at, size)], preferred_element_type=F32
        )

    whole = (2 * fe) // TILE
    lax.fori_loop(
        0, whole, lambda i, c: (project(pl.multiple_of(i * TILE, TILE), TILE), c)[1], 0
    )
    if 2 * fe > whole * TILE:
        project(whole * TILE, 2 * fe - whole * TILE)
    off = fe % LANES
    for at, size in cuts(up_to(fe, LANES), TILE):
        gate = hidden[:, at : at + size]
        up = hidden[:, fe - off + at : fe - off + at + size + LANES]
        if off:
            up = pltpu.roll(up, size + LANES - off, 1)
        up = up[:, :size]
        act[:, at : at + size] = ((up + 1.0) * gate * jax.nn.sigmoid(1.702 * gate)).astype(BF16)
    lane = lax.broadcasted_iota(jnp.int32, (rows, LANES), 1)
    expert = me // (n // EXPERTS)
    picked = (lane == free + expert) | (lane == free + EXPERTS + expert)
    share = jnp.sum(
        jnp.where(picked, tokens[:, last:dp].astype(F32), 0.0), axis=1, keepdims=True
    )

    pieces = cuts(d, 6 * LANES)

    def stage1(j):
        at, size = pieces[j]
        cols = pl.ds(at, size)
        result = (
            jnp.dot(act[:, 0:fe], w_out[:, cols], preferred_element_type=F32) * share
        )
        mine[:, cols] = result[:half]
        s1[:, cols] = result[half:].astype(BF16)
        span = pl.ds(at, up_to(size, LANES))
        send(s1.at[:, span], r1.at[:, span], s1_send.at[j], s1_recv.at[j], sibling)

    def stage2(j):
        at, size = pieces[j]
        cols = pl.ds(at, size)
        span = pl.ds(at, up_to(size, LANES))
        arrived(r1.at[:, span], s1_recv.at[j])
        total = mine[:, cols] + r1[:, cols].astype(F32)
        acc2[:, cols] = total[:quarter]
        s2[:, cols] = total[quarter:].astype(BF16)
        send(s2.at[:, span], r2.at[:, span], s2_send.at[j], s2_recv.at[j], across)

    def stage3(j):
        at, size = pieces[j]
        cols = pl.ds(at, size)
        span = pl.ds(at, up_to(size, LANES))
        arrived(r2.at[:, span], s2_recv.at[j])
        total = acc2[:, cols] + r2[:, cols].astype(F32)
        acc3[:, cols] = total[:count]
        s3[:, cols] = total.astype(BF16)
        for k in range(1, zs):
            there = pl.ds(k * count, count)
            index = j * (zs - 1) + k - 1
            send(
                s3.at[there, span], r3.at[there, span], s3_send.at[index], s3_recv.at[index], along(k)
            )

    def stage4(j):
        at, size = pieces[j]
        cols = pl.ds(at, size)
        span = pl.ds(at, up_to(size, LANES))
        total = acc3[:, cols]
        for k in range(1, zs):
            there = pl.ds(k * count, count)
            arrived(r3.at[there, span], s3_recv.at[j * (zs - 1) + k - 1])
            total = total + r3[there, cols].astype(F32)
        mix_ref[:, cols] = total.astype(BF16)

    for j in range(len(pieces)):
        stage1(j)
        if j:
            stage2(j - 1)
    stage2(len(pieces) - 1)
    steps = len(pieces)
    done = 0
    for g in range(groups // 2):
        attend(0, 2 * g, 2 * g + 2)
        upto = steps * (g + 1) // (groups // 2)
        for j in range(done, upto):
            stage3(j)
        done = upto
    store_early = pltpu.make_async_copy(
        o_buf.at[pl.ds(0, block)], att_hbm.at[pl.ds(0, block)], out_sem.at[1]
    )
    store_early.start()
    for j in range(steps):
        stage4(j)
    for copy in sent:
        copy.wait_send()
    store_late.wait()
    store_early.wait()


def on_device(
    n,
    query_proj,
    key_proj,
    value_proj,
    call_ids,
    sink_logits,
    routed_stream,
    expert_ids,
    route_weights,
    gate_up,
    down_proj,
):
    length = query_proj.shape[0]
    block = length // 2
    kv = key_proj.shape[1]
    count, d = routed_stream.shape
    dp = up_to(d + 2 * EXPERTS, LANES)
    fe = down_proj.shape[1]
    rows = n * count
    zs = n // 4
    wide = (fe // LANES) * LANES + up_to(fe, TILE) + LANES
    pieces = len(cuts(d, 6 * LANES))
    vmem = pl.BlockSpec(memory_space=pltpu.VMEM)
    smem = pl.BlockSpec(memory_space=pltpu.SMEM)
    hbm = pl.BlockSpec(memory_space=pl.ANY)
    dma = pltpu.SemaphoreType.DMA
    return pl.pallas_call(
        functools.partial(kernel, n),
        out_shape=(
            jax.ShapeDtypeStruct(query_proj.shape, BF16),
            jax.ShapeDtypeStruct(routed_stream.shape, BF16),
        ),
        in_specs=[hbm, hbm, hbm, vmem, smem, vmem, vmem, vmem, hbm, hbm],
        out_specs=(hbm, vmem),
        scratch_shapes=[
            pltpu.VMEM(query_proj.shape, BF16),
            pltpu.VMEM(query_proj.shape, BF16),
            pltpu.VMEM((WINDOW + length, kv), BF16),
            pltpu.VMEM((WINDOW + length, kv), BF16),
            pltpu.VMEM((8, WINDOW), jnp.int32),
            pltpu.VMEM((8, WINDOW), jnp.int32),
            pltpu.VMEM((2, block, WINDOW + block), F32),
            pltpu.VMEM((rows, dp), BF16),
            pltpu.VMEM(gate_up.shape[1:], BF16),
            pltpu.VMEM(down_proj.shape[1:], BF16),
            pltpu.VMEM((rows, wide), F32),
            pltpu.VMEM((rows, up_to(fe, TILE)), BF16),
            pltpu.VMEM((rows // 2, dp), F32),
            pltpu.VMEM((rows // 2, dp), BF16),
            pltpu.VMEM((rows // 2, dp), BF16),
            pltpu.VMEM((rows // 4, dp), F32),
            pltpu.VMEM((rows // 4, dp), BF16),
            pltpu.VMEM((rows // 4, dp), BF16),
            pltpu.VMEM((count, dp), F32),
            pltpu.VMEM((rows // 4, dp), BF16),
            pltpu.VMEM((rows // 4, dp), BF16),
            dma((4,)),
            dma((4,)),
            dma((2,)),
            dma((3,)),
            dma((3,)),
            dma((zs - 1,)),
            dma((zs,)),
            dma((2 * zs,)),
            dma((4 * zs,)),
            dma((pieces,)),
            dma((pieces,)),
            dma((pieces,)),
            dma((pieces,)),
            dma((pieces * (zs - 1),)),
            dma((pieces * (zs - 1),)),
            dma((2,)),
        ],
        compiler_params=pltpu.CompilerParams(
            collective_id=0, has_side_effects=True, vmem_limit_bytes=58 * 2**20
        ),
    )(
        query_proj,
        key_proj,
        value_proj,
        call_ids.reshape(1, length),
        sink_logits,
        routed_stream,
        expert_ids,
        route_weights,
        gate_up[0],
        down_proj[0],
    )


def solution(mesh):
    in_specs = (
        P(("groups", "ep"), None),
        P(("groups", "ep"), None),
        P(("groups", "ep"), None),
        P(("groups", "ep")),
        P(),
        P(("groups", "ep"), None),
        P(("groups", "ep"), None),
        P(("groups", "ep"), None),
        P("ep", None, None),
        P("ep", None, None),
    )
    out_specs = (P(("groups", "ep"), None), P(("groups", "ep"), None))
    return jax.shard_map(
        functools.partial(on_device, mesh.shape["ep"]),
        mesh=mesh,
        in_specs=in_specs,
        out_specs=out_specs,
        check_vma=False,
    )
```

```python
import functools

import jax
import jax.numpy as jnp
from jax import lax
from jax.experimental import pallas as pl
from jax.experimental.pallas import tpu as pltpu
from jax.sharding import PartitionSpec as P

HD = 64
WINDOW = 128
EXPERTS = 8
LANES = 128
TILE = 256
F32 = jnp.float32
BF16 = jnp.bfloat16


def up_to(value, unit):
    return -(-value // unit) * unit


def cuts(total, width):
    return [(at, min(width, total - at)) for at in range(0, total, width)]


def row_parts(rows, parts):
    step = up_to(-(-rows // parts), 16)
    return cuts(rows, step)


def kernel(
    n,
    q_hbm,
    k_hbm,
    v_hbm,
    calls_ref,
    sink_ref,
    routed_ref,
    ids_ref,
    route_ref,
    gate_hbm,
    down_hbm,
    o_buf,
    mix_ref,
    q_buf,
    k_cat,
    v_cat,
    calls_in,
    calls_out,
    bias,
    tokens,
    w_in,
    w_out,
    hidden,
    act,
    mine,
    s1,
    r1,
    acc2,
    s2,
    r2,
    acc3,
    s3,
    r3,
    load_sem,
    gate_sem,
    down_sem,
    halo_send,
    halo_recv,
    z_send,
    y_send,
    c_send,
    slot_recv,
    s1_send,
    s1_recv,
    s2_send,
    s2_recv,
    s3_send,
    s3_recv,
):
    zs = n // 4
    me = lax.axis_index("ep")
    core, row, z = me % 2, (me // 2) % 2, me // 4
    sibling = me + 1 - 2 * core
    across = me + 2 - 4 * row
    ahead, behind = (me + 1) % n, (me + n - 1) % n

    def along(by):
        return ((z + by) % zs) * 4 + row * 2 + core

    length = q_hbm.shape[0]
    block = length // 2
    count, d = routed_ref.shape
    dp = tokens.shape[1]
    fe = down_hbm.shape[0]
    half = zs * 2 * count
    quarter = zs * count

    barrier = pltpu.get_barrier_semaphore()
    for peer in [sibling, across, ahead, behind] + [along(k) for k in range(1, zs)]:
        pl.semaphore_signal(
            barrier, inc=1, device_id={"ep": peer}, device_id_type=pl.DeviceIdType.MESH
        )

    def remote(src, dst, send, recv, peer):
        return pltpu.make_async_remote_copy(
            src_ref=src,
            dst_ref=dst,
            send_sem=send,
            recv_sem=recv,
            device_id={"ep": peer},
            device_id_type=pl.DeviceIdType.MESH,
        )

    loads = [
        pltpu.make_async_copy(k_hbm, k_cat.at[pl.ds(WINDOW, length)], load_sem.at[0]),
        pltpu.make_async_copy(v_hbm, v_cat.at[pl.ds(WINDOW, length)], load_sem.at[1]),
        pltpu.make_async_copy(
            q_hbm.at[pl.ds(block, block)], q_buf.at[pl.ds(block, block)], load_sem.at[2]
        ),
        pltpu.make_async_copy(
            q_hbm.at[pl.ds(0, block)], q_buf.at[pl.ds(0, block)], load_sem.at[3]
        ),
    ]
    for copy in loads:
        copy.start()
    gate_loads = [
        pltpu.make_async_copy(
            gate_hbm.at[pl.ds(at, size)], w_in.at[pl.ds(at, size)], gate_sem.at[i]
        )
        for i, (at, size) in enumerate(row_parts(d, 4))
    ]
    down_loads = [
        pltpu.make_async_copy(
            down_hbm.at[pl.ds(at, size)], w_out.at[pl.ds(at, size)], down_sem.at[i]
        )
        for i, (at, size) in enumerate(row_parts(fe, 2))
    ]

    topk = ids_ref.shape[0]
    square = lax.broadcasted_iota(jnp.int32, (count, count), 0) == lax.broadcasted_iota(
        jnp.int32, (count, count), 1
    )
    ids = ids_ref[...].astype(F32)
    route = route_ref[...]

    def column(values, k):
        spread = jnp.broadcast_to(values[k : k + 1, :], (count, count))
        return jnp.sum(jnp.where(square, spread, 0.0), axis=1, keepdims=True)

    chosen = [(column(ids, k), column(route, k)) for k in range(topk)]
    lane = lax.broadcasted_iota(jnp.int32, (count, LANES), 1)
    last = dp - LANES
    free = d - last
    extra = jnp.zeros((count, LANES), F32)
    for e in range(EXPERTS):
        weight = sum(jnp.where(i == float(e), w, 0.0) for i, w in chosen)
        high = weight.astype(BF16).astype(F32)
        extra = jnp.where(lane == free + e, high, extra)
        extra = jnp.where(lane == free + EXPERTS + e, weight - high, extra)
    tokens[0:count, 0:d] = routed_ref[...]
    tail = tokens[0:count, last:dp].astype(F32)
    tokens[0:count, last:dp] = jnp.where(lane < free, tail, extra).astype(BF16)
    own_calls = calls_ref[...]
    calls_out[...] = jnp.broadcast_to(own_calls[:, length - WINDOW :], calls_out.shape)

    pl.semaphore_wait(barrier, zs + 3)

    def slot(cr, yr, zr):
        return tokens.at[pl.ds(((cr * 2 + yr) * zs + zr) * count, count)]

    def arrival(cr, yr, zr):
        return slot_recv.at[(cr * 2 + yr) * zs + zr]

    sent = []

    def send(*args):
        copy = remote(*args)
        copy.start()
        sent.append(copy)

    def arrived(ref, sem):
        pltpu.make_async_copy(ref, ref, sem).wait()

    for k in range(1, zs):
        send(slot(0, 0, 0), slot(0, 0, zs - k), z_send.at[k - 1], arrival(0, 0, zs - k), along(k))
    send(slot(0, 0, 0), slot(0, 1, 0), y_send.at[0], arrival(0, 1, 0), across)
    send(slot(0, 0, 0), slot(1, 0, 0), c_send.at[0], arrival(1, 0, 0), sibling)
    edge = pl.ds(length - WINDOW, WINDOW)
    head = pl.ds(0, WINDOW)
    send(k_hbm.at[edge], k_cat.at[head], halo_send.at[0], halo_recv.at[0], ahead)
    send(v_hbm.at[edge], v_cat.at[head], halo_send.at[1], halo_recv.at[1], ahead)
    send(calls_out, calls_in, halo_send.at[2], halo_recv.at[2], ahead)

    for copy in gate_loads + down_loads:
        copy.start()

    def make_bias(index, key_calls, query_calls, behind_ok):
        query = lax.broadcasted_iota(jnp.int32, (block, WINDOW + block), 0)
        key = lax.broadcasted_iota(jnp.int32, (block, WINDOW + block), 1)
        spread = jnp.broadcast_to(query_calls, (block, block))
        diag = lax.broadcasted_iota(jnp.int32, (block, block), 0) == lax.broadcasted_iota(
            jnp.int32, (block, block), 1
        )
        column = jnp.sum(
            jnp.where(diag, spread.astype(F32), 0.0), axis=1, keepdims=True
        ).astype(jnp.int32)
        seen = (key <= query + WINDOW) & (key > query) & (key_calls == column)
        if behind_ok is not None:
            seen = seen & ((key >= WINDOW) | behind_ok)
        bias[index] = jnp.where(seen, 0.0, -1e30)

    def attend(index, first, stop):
        base = index * block
        span = WINDOW + block

        def body(gp, carry):
            columns = pl.ds(pl.multiple_of(gp * LANES, LANES), LANES)
            k2 = k_cat[base : base + span, columns].astype(F32) * HD ** (-0.5)
            v2 = v_cat[base : base + span, columns].astype(F32)
            low = lax.broadcasted_iota(jnp.int32, (span, LANES), 1) < HD
            low_out = lax.broadcasted_iota(jnp.int32, (block, LANES), 1) < HD
            ones_low = jnp.where(low, 1.0, 0.0)
            ones_high = 1.0 - ones_low
            for side in range(2):
                keep = low if side == 0 else jnp.logical_not(low)
                ka = jnp.where(keep, k2, 0.0)
                kb = pltpu.roll(ka, HD, 1)
                va = jnp.where(keep, v2, 0.0)
                vb = pltpu.roll(va, HD, 1)
                if side:
                    ka, kb, va, vb = kb, ka, vb, va
                keys = jnp.concatenate([ka, kb], axis=0).astype(BF16)
                values = jnp.concatenate(
                    [
                        jnp.concatenate([va, ones_low], axis=1),
                        jnp.concatenate([vb, ones_high], axis=1),
                    ],
                    axis=0,
                ).astype(BF16)
                for pair in range(4):
                    at = pl.multiple_of(gp * (16 * HD) + (side * 8 + pair * 2) * HD, LANES)
                    q2 = q_buf[base : base + block, pl.ds(at, LANES)]
                    scores = lax.dot_general(
                        q2, keys, (((1,), (1,)), ((), ())), preferred_element_type=F32
                    )
                    seen = bias[index]
                    weights, sinks = [], []
                    for one in range(2):
                        sink = sink_ref[gp * 16 + side * 8 + pair * 2 + one]
                        part = scores[:, one * span : (one + 1) * span] + seen
                        largest = jnp.maximum(jnp.max(part, axis=1, keepdims=True), sink)
                        weights.append(jnp.exp(part - largest))
                        sinks.append(jnp.exp(sink - largest))
                    both = jnp.concatenate(weights, axis=1).astype(BF16)
                    mixed = jnp.dot(both, values, preferred_element_type=F32)
                    bottom = mixed[:, LANES:] + jnp.where(low_out, sinks[0], sinks[1])
                    o_buf[base : base + block, pl.ds(at, LANES)] = (
                        mixed[:, :LANES] / bottom
                    ).astype(BF16)
            return carry

        lax.fori_loop(first, stop, body, 0)

    groups = k_hbm.shape[1] // LANES
    make_bias(1, own_calls, own_calls[:, block:], None)
    for copy in loads[:3]:
        copy.wait()
    attend(1, 0, groups // 2)
    for k in range(1, zs):
        arrived(slot(0, 0, zs - k), arrival(0, 0, zs - k))
        send(slot(0, 0, zs - k), slot(0, 1, zs - k), y_send.at[k], arrival(0, 1, zs - k), across)
        send(slot(0, 0, zs - k), slot(1, 0, zs - k), c_send.at[k], arrival(1, 0, zs - k), sibling)
    attend(1, groups // 2, groups)
    for k in range(zs):
        zr = (zs - k) % zs
        arrived(slot(0, 1, zr), arrival(0, 1, zr))
        send(slot(0, 1, zr), slot(1, 1, zr), c_send.at[zs + k], arrival(1, 1, zr), sibling)
    for copy in gate_loads + down_loads:
        copy.wait()
    loads[3].wait()
    arrived(k_cat.at[head], halo_recv.at[0])
    arrived(v_cat.at[head], halo_recv.at[1])
    arrived(calls_in, halo_recv.at[2])
    make_bias(
        0,
        jnp.concatenate([calls_in[0:1, :], own_calls[:, :block]], axis=1),
        own_calls[:, :block],
        me > 0,
    )
    for yr in range(2):
        for zr in range(zs):
            arrived(slot(1, yr, zr), arrival(1, yr, zr))

    rows = n * count

    def project(at, size):
        hidden[:, pl.ds(at, size)] = jnp.dot(
            tokens[:, 0:d], w_in[:, pl.ds(at, size)], preferred_element_type=F32
        )

    whole = (2 * fe) // TILE
    lax.fori_loop(
        0, whole, lambda i, c: (project(pl.multiple_of(i * TILE, TILE), TILE), c)[1], 0
    )
    if 2 * fe > whole * TILE:
        project(whole * TILE, 2 * fe - whole * TILE)
    off = fe % LANES
    for at, size in cuts(up_to(fe, LANES), TILE):
        gate = hidden[:, at : at + size]
        up = hidden[:, fe - off + at : fe - off + at + size + LANES]
        if off:
            up = pltpu.roll(up, size + LANES - off, 1)
        up = up[:, :size]
        act[:, at : at + size] = ((up + 1.0) * gate * jax.nn.sigmoid(1.702 * gate)).astype(BF16)
    lane = lax.broadcasted_iota(jnp.int32, (rows, LANES), 1)
    expert = me // (n // EXPERTS)
    picked = (lane == free + expert) | (lane == free + EXPERTS + expert)
    share = jnp.sum(
        jnp.where(picked, tokens[:, last:dp].astype(F32), 0.0), axis=1, keepdims=True
    )

    pieces = cuts(d, 12 * LANES)

    def stage1(j):
        at, size = pieces[j]
        cols = pl.ds(at, size)
        result = (
            jnp.dot(act[:, 0:fe], w_out[:, cols], preferred_element_type=F32) * share
        )
        mine[:, cols] = result[:half]
        s1[:, cols] = result[half:].astype(BF16)
        span = pl.ds(at, up_to(size, LANES))
        send(s1.at[:, span], r1.at[:, span], s1_send.at[j], s1_recv.at[j], sibling)

    def stage2(j):
        at, size = pieces[j]
        cols = pl.ds(at, size)
        span = pl.ds(at, up_to(size, LANES))
        arrived(r1.at[:, span], s1_recv.at[j])
        total = mine[:, cols] + r1[:, cols].astype(F32)
        acc2[:, cols] = total[:quarter]
        s2[:, cols] = total[quarter:].astype(BF16)
        send(s2.at[:, span], r2.at[:, span], s2_send.at[j], s2_recv.at[j], across)

    def stage3(j):
        at, size = pieces[j]
        cols = pl.ds(at, size)
        span = pl.ds(at, up_to(size, LANES))
        arrived(r2.at[:, span], s2_recv.at[j])
        total = acc2[:, cols] + r2[:, cols].astype(F32)
        acc3[:, cols] = total[:count]
        s3[:, cols] = total.astype(BF16)
        for k in range(1, zs):
            there = pl.ds(k * count, count)
            index = j * (zs - 1) + k - 1
            send(
                s3.at[there, span], r3.at[there, span], s3_send.at[index], s3_recv.at[index], along(k)
            )

    def stage4(j):
        at, size = pieces[j]
        cols = pl.ds(at, size)
        span = pl.ds(at, up_to(size, LANES))
        total = acc3[:, cols]
        for k in range(1, zs):
            there = pl.ds(k * count, count)
            arrived(r3.at[there, span], s3_recv.at[j * (zs - 1) + k - 1])
            total = total + r3[there, cols].astype(F32)
        mix_ref[:, cols] = total.astype(BF16)

    for j in range(len(pieces)):
        stage1(j)
        if j:
            stage2(j - 1)
    stage2(len(pieces) - 1)
    steps = len(pieces)
    done = 0
    for g in range(groups // 2):
        attend(0, 2 * g, 2 * g + 2)
        upto = steps * (g + 1) // (groups // 2)
        for j in range(done, upto):
            stage3(j)
        done = upto
    for j in range(steps):
        stage4(j)
    for copy in sent:
        copy.wait_send()


def on_device(
    n,
    query_proj,
    key_proj,
    value_proj,
    call_ids,
    sink_logits,
    routed_stream,
    expert_ids,
    route_weights,
    gate_up,
    down_proj,
):
    length = query_proj.shape[0]
    block = length // 2
    kv = key_proj.shape[1]
    count, d = routed_stream.shape
    dp = up_to(d + 2 * EXPERTS, LANES)
    fe = down_proj.shape[1]
    rows = n * count
    zs = n // 4
    wide = (fe // LANES) * LANES + up_to(fe, TILE) + LANES
    pieces = len(cuts(d, 12 * LANES))
    vmem = pl.BlockSpec(memory_space=pltpu.VMEM)
    smem = pl.BlockSpec(memory_space=pltpu.SMEM)
    hbm = pl.BlockSpec(memory_space=pl.ANY)
    dma = pltpu.SemaphoreType.DMA
    return pl.pallas_call(
        functools.partial(kernel, n),
        out_shape=(
            pltpu.VMEM(query_proj.shape, BF16),
            pltpu.VMEM(routed_stream.shape, BF16),
        ),
        in_specs=[hbm, hbm, hbm, vmem, smem, vmem, vmem, vmem, hbm, hbm],
        out_specs=(vmem, vmem),
        scratch_shapes=[
            pltpu.VMEM(query_proj.shape, BF16),
            pltpu.VMEM((WINDOW + length, kv), BF16),
            pltpu.VMEM((WINDOW + length, kv), BF16),
            pltpu.VMEM((8, WINDOW), jnp.int32),
            pltpu.VMEM((8, WINDOW), jnp.int32),
            pltpu.VMEM((2, block, WINDOW + block), F32),
            pltpu.VMEM((rows, dp), BF16),
            pltpu.VMEM(gate_up.shape[1:], BF16),
            pltpu.VMEM(down_proj.shape[1:], BF16),
            pltpu.VMEM((rows, wide), F32),
            pltpu.VMEM((rows, up_to(fe, TILE)), BF16),
            pltpu.VMEM((rows // 2, dp), F32),
            pltpu.VMEM((rows // 2, dp), BF16),
            pltpu.VMEM((rows // 2, dp), BF16),
            pltpu.VMEM((rows // 4, dp), F32),
            pltpu.VMEM((rows // 4, dp), BF16),
            pltpu.VMEM((rows // 4, dp), BF16),
            pltpu.VMEM((count, dp), F32),
            pltpu.VMEM((rows // 4, dp), BF16),
            pltpu.VMEM((rows // 4, dp), BF16),
            dma((4,)),
            dma((4,)),
            dma((2,)),
            dma((3,)),
            dma((3,)),
            dma((zs - 1,)),
            dma((zs,)),
            dma((2 * zs,)),
            dma((4 * zs,)),
            dma((pieces,)),
            dma((pieces,)),
            dma((pieces,)),
            dma((pieces,)),
            dma((pieces * (zs - 1),)),
            dma((pieces * (zs - 1),)),
        ],
        compiler_params=pltpu.CompilerParams(
            collective_id=0, has_side_effects=True, vmem_limit_bytes=58 * 2**20
        ),
    )(
        query_proj,
        key_proj,
        value_proj,
        call_ids.reshape(1, length),
        sink_logits,
        routed_stream,
        expert_ids.T,
        route_weights.T,
        gate_up[0],
        down_proj[0],
    )


def solution(mesh):
    in_specs = (
        P(("groups", "ep"), None),
        P(("groups", "ep"), None),
        P(("groups", "ep"), None),
        P(("groups", "ep")),
        P(),
        P(("groups", "ep"), None),
        P(("groups", "ep"), None),
        P(("groups", "ep"), None),
        P("ep", None, None),
        P("ep", None, None),
    )
    out_specs = (P(("groups", "ep"), None), P(("groups", "ep"), None))
    return jax.shard_map(
        functools.partial(on_device, mesh.shape["ep"]),
        mesh=mesh,
        in_specs=in_specs,
        out_specs=out_specs,
        check_vma=False,
    )
```

```python
import functools

import jax
import jax.numpy as jnp
from jax import lax
from jax.experimental import pallas as pl
from jax.experimental.pallas import tpu as pltpu
from jax.sharding import PartitionSpec as P

HD = 64
WINDOW = 128
EXPERTS = 8
LANES = 128
TILE = 256
F32 = jnp.float32
BF16 = jnp.bfloat16


def up_to(value, unit):
    return -(-value // unit) * unit


def cuts(total, width):
    return [(at, min(width, total - at)) for at in range(0, total, width)]


def row_parts(rows, parts):
    step = up_to(-(-rows // parts), 16)
    return cuts(rows, step)


def kernel(
    n,
    q_hbm,
    k_hbm,
    v_hbm,
    calls_ref,
    sink_ref,
    routed_ref,
    ids_ref,
    route_ref,
    gate_hbm,
    down_hbm,
    o_buf,
    mix_ref,
    q_buf,
    k_cat,
    v_cat,
    calls_in,
    calls_out,
    bias,
    tokens,
    w_in,
    w_out,
    hidden,
    act,
    mine,
    s1,
    r1,
    acc2,
    s2,
    r2,
    acc3,
    s3,
    r3,
    load_sem,
    gate_sem,
    down_sem,
    halo_send,
    halo_recv,
    z_send,
    y_send,
    c_send,
    slot_recv,
    s1_send,
    s1_recv,
    s2_send,
    s2_recv,
    s3_send,
    s3_recv,
):
    zs = n // 4
    me = lax.axis_index("ep")
    core, row, z = me % 2, (me // 2) % 2, me // 4
    sibling = me + 1 - 2 * core
    across = me + 2 - 4 * row
    ahead, behind = (me + 1) % n, (me + n - 1) % n

    def along(by):
        return ((z + by) % zs) * 4 + row * 2 + core

    length = q_hbm.shape[0]
    block = length // 2
    count, d = routed_ref.shape
    dp = tokens.shape[1]
    fe = down_hbm.shape[0]
    half = zs * 2 * count
    quarter = zs * count

    barrier = pltpu.get_barrier_semaphore()
    for peer in [sibling, across, ahead, behind] + [along(k) for k in range(1, zs)]:
        pl.semaphore_signal(
            barrier, inc=1, device_id={"ep": peer}, device_id_type=pl.DeviceIdType.MESH
        )

    def remote(src, dst, send, recv, peer):
        return pltpu.make_async_remote_copy(
            src_ref=src,
            dst_ref=dst,
            send_sem=send,
            recv_sem=recv,
            device_id={"ep": peer},
            device_id_type=pl.DeviceIdType.MESH,
        )

    loads = [
        pltpu.make_async_copy(k_hbm, k_cat.at[pl.ds(WINDOW, length)], load_sem.at[0]),
        pltpu.make_async_copy(v_hbm, v_cat.at[pl.ds(WINDOW, length)], load_sem.at[1]),
        pltpu.make_async_copy(
            q_hbm.at[pl.ds(block, block)], q_buf.at[pl.ds(block, block)], load_sem.at[2]
        ),
        pltpu.make_async_copy(
            q_hbm.at[pl.ds(0, block)], q_buf.at[pl.ds(0, block)], load_sem.at[3]
        ),
    ]
    for copy in loads:
        copy.start()
    gate_loads = [
        pltpu.make_async_copy(
            gate_hbm.at[pl.ds(at, size)], w_in.at[pl.ds(at, size)], gate_sem.at[i]
        )
        for i, (at, size) in enumerate(row_parts(d, 4))
    ]
    down_loads = [
        pltpu.make_async_copy(
            down_hbm.at[pl.ds(at, size)], w_out.at[pl.ds(at, size)], down_sem.at[i]
        )
        for i, (at, size) in enumerate(row_parts(fe, 2))
    ]

    topk = ids_ref.shape[0]
    square = lax.broadcasted_iota(jnp.int32, (count, count), 0) == lax.broadcasted_iota(
        jnp.int32, (count, count), 1
    )
    ids = ids_ref[...].astype(F32)
    route = route_ref[...]

    def column(values, k):
        spread = jnp.broadcast_to(values[k : k + 1, :], (count, count))
        return jnp.sum(jnp.where(square, spread, 0.0), axis=1, keepdims=True)

    chosen = [(column(ids, k), column(route, k)) for k in range(topk)]
    lane = lax.broadcasted_iota(jnp.int32, (count, LANES), 1)
    last = dp - LANES
    free = d - last
    extra = jnp.zeros((count, LANES), F32)
    for e in range(EXPERTS):
        weight = sum(jnp.where(i == float(e), w, 0.0) for i, w in chosen)
        high = weight.astype(BF16).astype(F32)
        extra = jnp.where(lane == free + e, high, extra)
        extra = jnp.where(lane == free + EXPERTS + e, weight - high, extra)
    tokens[0:count, 0:d] = routed_ref[...]
    tail = tokens[0:count, last:dp].astype(F32)
    tokens[0:count, last:dp] = jnp.where(lane < free, tail, extra).astype(BF16)
    own_calls = calls_ref[...]
    calls_out[...] = jnp.broadcast_to(own_calls[:, length - WINDOW :], calls_out.shape)

    pl.semaphore_wait(barrier, zs + 3)

    def slot(cr, yr, zr):
        return tokens.at[pl.ds(((cr * 2 + yr) * zs + zr) * count, count)]

    def arrival(cr, yr, zr):
        return slot_recv.at[(cr * 2 + yr) * zs + zr]

    sent = []

    def send(*args):
        copy = remote(*args)
        copy.start()
        sent.append(copy)

    def arrived(ref, sem):
        pltpu.make_async_copy(ref, ref, sem).wait()

    for k in range(1, zs):
        send(slot(0, 0, 0), slot(0, 0, zs - k), z_send.at[k - 1], arrival(0, 0, zs - k), along(k))
    send(slot(0, 0, 0), slot(0, 1, 0), y_send.at[0], arrival(0, 1, 0), across)
    send(slot(0, 0, 0), slot(1, 0, 0), c_send.at[0], arrival(1, 0, 0), sibling)
    edge = pl.ds(length - WINDOW, WINDOW)
    head = pl.ds(0, WINDOW)
    send(k_hbm.at[edge], k_cat.at[head], halo_send.at[0], halo_recv.at[0], ahead)
    send(v_hbm.at[edge], v_cat.at[head], halo_send.at[1], halo_recv.at[1], ahead)
    send(calls_out, calls_in, halo_send.at[2], halo_recv.at[2], ahead)

    for copy in gate_loads + down_loads:
        copy.start()

    def make_bias(index, key_calls, query_calls, behind_ok):
        query = lax.broadcasted_iota(jnp.int32, (block, WINDOW + block), 0)
        key = lax.broadcasted_iota(jnp.int32, (block, WINDOW + block), 1)
        spread = jnp.broadcast_to(query_calls, (block, block))
        diag = lax.broadcasted_iota(jnp.int32, (block, block), 0) == lax.broadcasted_iota(
            jnp.int32, (block, block), 1
        )
        column = jnp.sum(
            jnp.where(diag, spread.astype(F32), 0.0), axis=1, keepdims=True
        ).astype(jnp.int32)
        seen = (key <= query + WINDOW) & (key > query) & (key_calls == column)
        if behind_ok is not None:
            seen = seen & ((key >= WINDOW) | behind_ok)
        bias[index] = jnp.where(seen, 0.0, -1e30)

    def attend(index, first, stop):
        base = index * block
        span = WINDOW + block

        def body(gp, carry):
            columns = pl.ds(pl.multiple_of(gp * LANES, LANES), LANES)
            k2 = k_cat[base : base + span, columns].astype(F32) * HD ** (-0.5)
            v2 = v_cat[base : base + span, columns].astype(F32)
            low = lax.broadcasted_iota(jnp.int32, (span, LANES), 1) < HD
            low_out = lax.broadcasted_iota(jnp.int32, (block, LANES), 1) < HD
            ones_low = jnp.where(low, 1.0, 0.0)
            ones_high = 1.0 - ones_low
            for side in range(2):
                keep = low if side == 0 else jnp.logical_not(low)
                ka = jnp.where(keep, k2, 0.0)
                kb = pltpu.roll(ka, HD, 1)
                va = jnp.where(keep, v2, 0.0)
                vb = pltpu.roll(va, HD, 1)
                if side:
                    ka, kb, va, vb = kb, ka, vb, va
                keys = jnp.concatenate([ka, kb], axis=0).astype(BF16)
                values = jnp.concatenate(
                    [
                        jnp.concatenate([va, ones_low], axis=1),
                        jnp.concatenate([vb, ones_high], axis=1),
                    ],
                    axis=0,
                ).astype(BF16)
                for pair in range(4):
                    at = pl.multiple_of(gp * (16 * HD) + (side * 8 + pair * 2) * HD, LANES)
                    q2 = q_buf[base : base + block, pl.ds(at, LANES)]
                    scores = lax.dot_general(
                        q2, keys, (((1,), (1,)), ((), ())), preferred_element_type=F32
                    )
                    seen = bias[index]
                    weights, sinks = [], []
                    for one in range(2):
                        sink = sink_ref[gp * 16 + side * 8 + pair * 2 + one]
                        part = scores[:, one * span : (one + 1) * span] + seen
                        largest = jnp.maximum(jnp.max(part, axis=1, keepdims=True), sink)
                        weights.append(jnp.exp(part - largest))
                        sinks.append(jnp.exp(sink - largest))
                    both = jnp.concatenate(weights, axis=1).astype(BF16)
                    mixed = jnp.dot(both, values, preferred_element_type=F32)
                    bottom = mixed[:, LANES:] + jnp.where(low_out, sinks[0], sinks[1])
                    o_buf[base : base + block, pl.ds(at, LANES)] = (
                        mixed[:, :LANES] / bottom
                    ).astype(BF16)
            return carry

        lax.fori_loop(first, stop, body, 0)

    groups = k_hbm.shape[1] // LANES
    make_bias(1, own_calls, own_calls[:, block:], None)
    for copy in loads[:3]:
        copy.wait()
    attend(1, 0, groups // 2)
    for k in range(1, zs):
        arrived(slot(0, 0, zs - k), arrival(0, 0, zs - k))
        send(slot(0, 0, zs - k), slot(0, 1, zs - k), y_send.at[k], arrival(0, 1, zs - k), across)
        send(slot(0, 0, zs - k), slot(1, 0, zs - k), c_send.at[k], arrival(1, 0, zs - k), sibling)
    attend(1, groups // 2, groups)
    for k in range(zs):
        zr = (zs - k) % zs
        arrived(slot(0, 1, zr), arrival(0, 1, zr))
        send(slot(0, 1, zr), slot(1, 1, zr), c_send.at[zs + k], arrival(1, 1, zr), sibling)
    for copy in gate_loads + down_loads:
        copy.wait()
    for yr in range(2):
        for zr in range(zs):
            arrived(slot(1, yr, zr), arrival(1, yr, zr))

    rows = n * count

    def project(at, size):
        hidden[:, pl.ds(at, size)] = jnp.dot(
            tokens[:, 0:d], w_in[:, pl.ds(at, size)], preferred_element_type=F32
        )

    whole = (2 * fe) // TILE
    lax.fori_loop(
        0, whole, lambda i, c: (project(pl.multiple_of(i * TILE, TILE), TILE), c)[1], 0
    )
    if 2 * fe > whole * TILE:
        project(whole * TILE, 2 * fe - whole * TILE)
    off = fe % LANES
    for at, size in cuts(up_to(fe, LANES), TILE):
        gate = hidden[:, at : at + size]
        up = hidden[:, fe - off + at : fe - off + at + size + LANES]
        if off:
            up = pltpu.roll(up, size + LANES - off, 1)
        up = up[:, :size]
        act[:, at : at + size] = ((up + 1.0) * gate * jax.nn.sigmoid(1.702 * gate)).astype(BF16)
    lane = lax.broadcasted_iota(jnp.int32, (rows, LANES), 1)
    expert = me // (n // EXPERTS)
    picked = (lane == free + expert) | (lane == free + EXPERTS + expert)
    share = jnp.sum(
        jnp.where(picked, tokens[:, last:dp].astype(F32), 0.0), axis=1, keepdims=True
    )

    pieces = cuts(d, 12 * LANES)

    def stage1(j):
        at, size = pieces[j]
        cols = pl.ds(at, size)
        result = (
            jnp.dot(act[:, 0:fe], w_out[:, cols], preferred_element_type=F32) * share
        )
        mine[:, cols] = result[:half]
        s1[:, cols] = result[half:].astype(BF16)
        span = pl.ds(at, up_to(size, LANES))
        send(s1.at[:, span], r1.at[:, span], s1_send.at[j], s1_recv.at[j], sibling)

    def stage2(j):
        at, size = pieces[j]
        cols = pl.ds(at, size)
        span = pl.ds(at, up_to(size, LANES))
        arrived(r1.at[:, span], s1_recv.at[j])
        total = mine[:, cols] + r1[:, cols].astype(F32)
        acc2[:, cols] = total[:quarter]
        s2[:, cols] = total[quarter:].astype(BF16)
        send(s2.at[:, span], r2.at[:, span], s2_send.at[j], s2_recv.at[j], across)

    def stage3(j):
        at, size = pieces[j]
        cols = pl.ds(at, size)
        span = pl.ds(at, up_to(size, LANES))
        arrived(r2.at[:, span], s2_recv.at[j])
        total = acc2[:, cols] + r2[:, cols].astype(F32)
        acc3[:, cols] = total[:count]
        s3[:, cols] = total.astype(BF16)
        for k in range(1, zs):
            there = pl.ds(k * count, count)
            index = j * (zs - 1) + k - 1
            send(
                s3.at[there, span], r3.at[there, span], s3_send.at[index], s3_recv.at[index], along(k)
            )

    def stage4(j):
        at, size = pieces[j]
        cols = pl.ds(at, size)
        span = pl.ds(at, up_to(size, LANES))
        total = acc3[:, cols]
        for k in range(1, zs):
            there = pl.ds(k * count, count)
            arrived(r3.at[there, span], s3_recv.at[j * (zs - 1) + k - 1])
            total = total + r3[there, cols].astype(F32)
        mix_ref[:, cols] = total.astype(BF16)

    for j in range(len(pieces)):
        stage1(j)
        if j:
            stage2(j - 1)
    stage2(len(pieces) - 1)
    loads[3].wait()
    arrived(k_cat.at[head], halo_recv.at[0])
    arrived(v_cat.at[head], halo_recv.at[1])
    arrived(calls_in, halo_recv.at[2])
    make_bias(
        0,
        jnp.concatenate([calls_in[0:1, :], own_calls[:, :block]], axis=1),
        own_calls[:, :block],
        me > 0,
    )
    steps = len(pieces)
    done = 0
    for g in range(groups // 2):
        attend(0, 2 * g, 2 * g + 2)
        upto = steps * (g + 1) // (groups // 2)
        for j in range(done, upto):
            stage3(j)
        done = upto
    for j in range(steps):
        stage4(j)
    for copy in sent:
        copy.wait_send()


def on_device(
    n,
    query_proj,
    key_proj,
    value_proj,
    call_ids,
    sink_logits,
    routed_stream,
    expert_ids,
    route_weights,
    gate_up,
    down_proj,
):
    length = query_proj.shape[0]
    block = length // 2
    kv = key_proj.shape[1]
    count, d = routed_stream.shape
    dp = up_to(d + 2 * EXPERTS, LANES)
    fe = down_proj.shape[1]
    rows = n * count
    zs = n // 4
    wide = (fe // LANES) * LANES + up_to(fe, TILE) + LANES
    pieces = len(cuts(d, 12 * LANES))
    vmem = pl.BlockSpec(memory_space=pltpu.VMEM)
    smem = pl.BlockSpec(memory_space=pltpu.SMEM)
    hbm = pl.BlockSpec(memory_space=pl.ANY)
    dma = pltpu.SemaphoreType.DMA
    return pl.pallas_call(
        functools.partial(kernel, n),
        out_shape=(
            pltpu.VMEM(query_proj.shape, BF16),
            pltpu.VMEM(routed_stream.shape, BF16),
        ),
        in_specs=[hbm, hbm, hbm, vmem, smem, vmem, vmem, vmem, hbm, hbm],
        out_specs=(vmem, vmem),
        scratch_shapes=[
            pltpu.VMEM(query_proj.shape, BF16),
            pltpu.VMEM((WINDOW + length, kv), BF16),
            pltpu.VMEM((WINDOW + length, kv), BF16),
            pltpu.VMEM((8, WINDOW), jnp.int32),
            pltpu.VMEM((8, WINDOW), jnp.int32),
            pltpu.VMEM((2, block, WINDOW + block), F32),
            pltpu.VMEM((rows, dp), BF16),
            pltpu.VMEM(gate_up.shape[1:], BF16),
            pltpu.VMEM(down_proj.shape[1:], BF16),
            pltpu.VMEM((rows, wide), F32),
            pltpu.VMEM((rows, up_to(fe, TILE)), BF16),
            pltpu.VMEM((rows // 2, dp), F32),
            pltpu.VMEM((rows // 2, dp), BF16),
            pltpu.VMEM((rows // 2, dp), BF16),
            pltpu.VMEM((rows // 4, dp), F32),
            pltpu.VMEM((rows // 4, dp), BF16),
            pltpu.VMEM((rows // 4, dp), BF16),
            pltpu.VMEM((count, dp), F32),
            pltpu.VMEM((rows // 4, dp), BF16),
            pltpu.VMEM((rows // 4, dp), BF16),
            dma((4,)),
            dma((4,)),
            dma((2,)),
            dma((3,)),
            dma((3,)),
            dma((zs - 1,)),
            dma((zs,)),
            dma((2 * zs,)),
            dma((4 * zs,)),
            dma((pieces,)),
            dma((pieces,)),
            dma((pieces,)),
            dma((pieces,)),
            dma((pieces * (zs - 1),)),
            dma((pieces * (zs - 1),)),
        ],
        compiler_params=pltpu.CompilerParams(
            collective_id=0, has_side_effects=True, vmem_limit_bytes=58 * 2**20
        ),
    )(
        query_proj,
        key_proj,
        value_proj,
        call_ids.reshape(1, length),
        sink_logits,
        routed_stream,
        expert_ids.T,
        route_weights.T,
        gate_up[0],
        down_proj[0],
    )


def solution(mesh):
    in_specs = (
        P(("groups", "ep"), None),
        P(("groups", "ep"), None),
        P(("groups", "ep"), None),
        P(("groups", "ep")),
        P(),
        P(("groups", "ep"), None),
        P(("groups", "ep"), None),
        P(("groups", "ep"), None),
        P("ep", None, None),
        P("ep", None, None),
    )
    out_specs = (P(("groups", "ep"), None), P(("groups", "ep"), None))
    return jax.shard_map(
        functools.partial(on_device, mesh.shape["ep"]),
        mesh=mesh,
        in_specs=in_specs,
        out_specs=out_specs,
        check_vma=False,
    )
```
